32 devices in a mesh: fsdp: 8 (over z, y), ctx: 2 (over x), tp: 2 (over core).
Axes of the slice: x: 2, y: 2, z: 4, core: 2. Of those that a mesh axis runs over, the one named last changes fastest.
Arguments:
- tokens: bfloat16 [2, 8192, 768], P(None, ('fsdp', 'ctx')), may hold values from -6 to 6
- gain_attn: bfloat16 [768], P('fsdp'), may hold values from 0.099609375 to 1.8984375
- w_query: bfloat16 [768, 768], P('fsdp', 'tp'), may hold values from -0.21875 to 0.21875
- w_key: bfloat16 [768, 768], P('fsdp', 'tp'), may hold values from -0.21875 to 0.21875
- w_value: bfloat16 [768, 768], P('fsdp', 'tp'), may hold values from -0.21875 to 0.21875
- w_out: bfloat16 [768, 768], P('tp', 'fsdp'), may hold values from -6 to 6
- gain_ffn: bfloat16 [768], P('fsdp'), may hold values from 0.099609375 to 1.8984375
- w_gate: bfloat16 [768, 1152], P('fsdp', 'tp'), may hold values from -0.21875 to 0.21875
- w_up: bfloat16 [768, 1152], P('fsdp', 'tp'), may hold values from -0.21875 to 0.21875
- w_down: bfloat16 [1152, 768], P('tp', 'fsdp'), may hold values from -0.1875 to 0.1875
- cotangent: bfloat16 [2, 8192, 768], P(None, ('fsdp', 'ctx')), may hold values from -6 to 6
Outputs:
- output: bfloat16 [2, 8192, 768], P(None, ('fsdp', 'ctx'))
- grad_tokens: float32 [2, 8192, 768], P(None, ('fsdp', 'ctx'))
- grad_gain_attn: float32 [768], P('fsdp')
- grad_query: float32 [768, 768], P('fsdp', 'tp')
- grad_key: float32 [768, 768], P('fsdp', 'tp')
- grad_value: float32 [768, 768], P('fsdp', 'tp')
- grad_out: float32 [768, 768], P('tp', 'fsdp')
- grad_gain_ffn: float32 [768], P('fsdp')
- grad_gate: float32 [768, 1152], P('fsdp', 'tp')
- grad_up: float32 [768, 1152], P('fsdp', 'tp')
- grad_down: float32 [1152, 768], P('tp', 'fsdp')
The draws below stay inside these ranges and needn't reach their ends.
All inputs are finite; a program needn't handle non-finite values.
Results may differ from the reference program's by a relative error of at most 0.025.
Values may be sent and summed in bfloat16 or wider, within the bound.
A program may use at most 192 MiB of HBM per device.

```python
import jax
import jax.numpy as jnp
from jax import lax

D = 768
HEADS = 12
HD = 64
FF = 1152
SLOTS = 2
LEN = 1024
SEQS = 16
N_FSDP = 8


def spiked(entries, key, source, target, shards_of, factor):
    def block_of(dim):
        return (jnp.arange(entries.shape[dim]) // (entries.shape[dim] // shards_of)).reshape((-1,) + (1,) * (entries.ndim - 1 - dim))

    first = jax.random.permutation(key, shards_of)[block_of(target)]
    far = (block_of(target) + shards_of // 2) % shards_of
    return jnp.where((block_of(source) == first) | (block_of(source) == far), factor * entries, entries)


def steps_of(own_key, extent, shards, smallest, high):
    loudness = 1.0
    for dim, blocks in shards:
        draws = jax.random.uniform(jax.random.fold_in(jax.random.fold_in(own_key, 6), dim), (blocks,), jnp.float32, smallest / len(shards), high / len(shards))
        loudness = loudness * jnp.repeat(jnp.exp(draws), extent[dim] // blocks).reshape((-1,) + (1,) * (len(extent) - 1 - dim))
    return loudness


def normal_values(own_key, dims, deviation, bound, pieces=(), held_as=jnp.bfloat16):
    drawn = jax.random.normal(own_key, dims, jnp.float32) * deviation
    if len(pieces) > 0:
        drawn = steps_of(own_key, dims, pieces, -0.22, 0.18) * drawn
    return jnp.clip(drawn, min=-bound, max=bound).astype(held_as)


def heavy_noise(stream_key, shape, spread, bound, shards, heavy, kind=jnp.bfloat16):
    values = spread * jax.random.normal(stream_key, shape, jnp.float32)
    if shards:
        values = values * steps_of(stream_key, shape, shards, -0.22, 0.18)
    return jnp.clip(spiked(values, jax.random.fold_in(stream_key, 3), *heavy), -bound, bound).astype(kind)


def setup_inputs(seed: int = 0) -> dict:
    keys = jax.random.split(jax.random.key(seed), 12)
    return {
        "tokens": normal_values(keys[0], (SLOTS, N_FSDP * LEN, D), 1.0, 6.0, ((1, 16),)),
        "gain_attn": jnp.clip(1.0 + 0.18 * jax.random.normal(keys[1], (D,), jnp.float32), 0.099609375, 1.8984375).astype(jnp.bfloat16),
        "w_query": normal_values(keys[2], (D, D), D ** -0.5, 0.21875, ((0, 8), (1, 2))),
        "w_key": normal_values(keys[3], (D, D), D ** -0.5, 0.21875, ((0, 8), (1, 2))),
        "w_value": normal_values(keys[4], (D, D), D ** -0.5, 0.21875, ((0, 8), (1, 2))),
        "w_out": normal_values(keys[5], (D, D), 1.0, 6.0, ((0, 2), (1, 8))),
        "gain_ffn": jnp.clip(1.0 + 0.18 * jax.random.normal(keys[6], (D,), jnp.float32), 0.099609375, 1.8984375).astype(jnp.bfloat16),
        "w_gate": normal_values(keys[7], (D, FF), D ** -0.5, 0.21875, ((0, 8), (1, 2))),
        "w_up": normal_values(keys[8], (D, FF), D ** -0.5, 0.21875, ((0, 8), (1, 2))),
        "w_down": normal_values(keys[9], (FF, D), FF ** -0.5, 0.1875, ((0, 2), (1, 8))),
        "cotangent": heavy_noise(keys[10], (SLOTS, N_FSDP * LEN, D), 1.0, 6.0, ((1, 16),), (1, 2, 16, 2.0)),
    }


eps_norm = 1e-05
rope_base = 160000.0

@jax.custom_vjp
def low(v):
    return lax.optimization_barrier(v.astype(jnp.bfloat16)).astype(jnp.float32)

@jax.custom_vjp
def low_back(v):
    return v

def low_keep(v):
    return (low(v), None)

def low_pass(kept, grad):
    return (grad,)

def back_keep(v):
    return (v, None)

def back_low(kept, grad):
    return (low(grad),)
low.defvjp(low_keep, low_pass)
low_back.defvjp(back_keep, back_low)

def layer_norm(x):
    mean = lax.optimization_barrier(jnp.mean(x, axis=-1, keepdims=True))
    centred = x - mean
    var = lax.optimization_barrier(jnp.mean(centred * centred, axis=-1, keepdims=True))
    return centred * lax.rsqrt(var + eps_norm)

def matmul(a, b):
    return jnp.dot(a, b, precision=lax.Precision.HIGHEST, preferred_element_type=jnp.float32)

def rope_angles(length):
    position = jnp.arange(length, dtype=jnp.int32).astype(jnp.float32)
    inverse = 1.0 / rope_base ** (jnp.arange(0, HD, 2, dtype=jnp.int32).astype(jnp.float32) / HD)
    angle = position[:, None] * inverse[None, :]
    angle = jnp.concatenate([angle, angle], axis=-1)
    return (jnp.cos(angle), jnp.sin(angle))

def rotate(heads, cosine, sine):
    half = heads.shape[-1] // 2
    turned = jnp.concatenate([-heads[..., half:], heads[..., :half]], axis=-1)
    return heads * cosine[:, None, :] + turned * sine[:, None, :]

def layer(x, gain_attn, w_query, w_key, w_value, w_out, gain_ffn, w_gate, w_up, w_down):
    cosine, sine = rope_angles(LEN)
    scale = HD ** (-0.5)
    h1 = low(layer_norm(x) * gain_attn)
    query = low(rotate(low_back(matmul(h1, w_query)).reshape(LEN, HEADS, HD), cosine, sine))
    key = low(rotate(low_back(matmul(h1, w_key)).reshape(LEN, HEADS, HD), cosine, sine))
    value = low(low_back(matmul(h1, w_value))).reshape(LEN, HEADS, HD)
    scores = low_back(jnp.einsum('qhd,khd->hqk', query, key, precision=lax.Precision.HIGHEST) * scale)
    shifted = jnp.exp(scores - lax.optimization_barrier(jnp.max(scores, axis=-1, keepdims=True)))
    probs = low(shifted / lax.optimization_barrier(jnp.sum(shifted, axis=-1, keepdims=True)))
    attended = jnp.einsum('hqk,khd->qhd', probs, value, precision=lax.Precision.HIGHEST)
    attended = low(low_back(attended)).reshape(LEN, D)
    x2 = x + low_back(matmul(attended, w_out))
    h2 = low(layer_norm(x2) * gain_ffn)
    gate = low_back(matmul(h2, w_gate))
    up_part = low_back(matmul(h2, w_up))
    hidden = low(jax.nn.gelu(gate, approximate=False) * up_part)
    return x2 + low_back(matmul(hidden, w_down))

def reference(tokens, gain_attn, w_query, w_key, w_value, w_out, gain_ffn, w_gate, w_up, w_down, cotangent):
    weights = tuple((w.astype(jnp.float32) for w in (gain_attn, w_query, w_key, w_value, w_out, gain_ffn, w_gate, w_up, w_down)))
    inputs = tokens.astype(jnp.float32).reshape(SEQS, LEN, D)
    cotans = cotangent.astype(jnp.float32).reshape(SEQS, LEN, D)

    def one_sequence(totals, pair):
        x, grad_y = pair
        result, back = jax.vjp(layer, x, *weights)
        grads = back(grad_y)
        totals = tuple((t + g for t, g in zip(totals, grads[1:])))
        return (totals, (result.astype(jnp.bfloat16), grads[0]))
    zeros = tuple((jnp.zeros_like(w) for w in weights))
    totals, (outputs, grad_inputs) = lax.scan(one_sequence, zeros, (inputs, cotans))
    whole_shape = (SLOTS, N_FSDP * LEN, D)
    return (outputs.reshape(whole_shape), grad_inputs.reshape(whole_shape), totals[0], totals[1], totals[2], totals[3], totals[4], totals[5], totals[6], totals[7], totals[8])
```

```python
from functools import partial

import jax
import jax.numpy as jnp
import numpy as np
from jax import lax
from jax.experimental import pallas as pl
from jax.experimental.pallas import tpu as pltpu
from jax.sharding import PartitionSpec as P

HD = 64


eps_norm = 1e-05
rope_base = 160000.0


def layer_norm(x):
    mean = jnp.mean(x, axis=-1, keepdims=True)
    centred = x - mean
    var = jnp.mean(centred * centred, axis=-1, keepdims=True)
    rstd = lax.rsqrt(var + eps_norm)
    return (centred * rstd, rstd)


def norm_back(grad_normed, normed, rstd):
    first = jnp.mean(grad_normed, axis=-1, keepdims=True)
    second = jnp.mean(grad_normed * normed, axis=-1, keepdims=True)
    return rstd * (grad_normed - first - normed * second)


def rope_angles(first, count, width):
    position = (first + jnp.arange(count, dtype=jnp.int32)).astype(jnp.float32)
    inverse = 1.0 / rope_base ** (
        jnp.arange(0, width, 2, dtype=jnp.int32).astype(jnp.float32) / width
    )
    angle = position[:, None] * inverse[None, :]
    angle = jnp.concatenate([angle, angle], axis=-1)
    return (jnp.cos(angle), jnp.sin(angle))


def rotate(heads, cosine, sine, sign):
    half = heads.shape[-1] // 2
    turned = jnp.concatenate([-heads[..., half:], heads[..., :half]], axis=-1)
    return heads * cosine[:, None, :] + sign * turned * sine[:, None, :]


def matmul(a, b):
    return jnp.dot(a, b, preferred_element_type=jnp.float32)


def on_device_blocks(
    tokens, gain_attn, w_query, w_key, w_value, w_out, gain_ffn, w_gate, w_up, w_down, cotangent
):
    full = (
        lax.all_gather(gain_attn, "fsdp", axis=0, tiled=True),
        lax.all_gather(w_query, "fsdp", axis=0, tiled=True),
        lax.all_gather(w_key, "fsdp", axis=0, tiled=True),
        lax.all_gather(w_value, "fsdp", axis=0, tiled=True),
        lax.all_gather(w_out, "fsdp", axis=1, tiled=True),
        lax.all_gather(gain_ffn, "fsdp", axis=0, tiled=True),
        lax.all_gather(w_gate, "fsdp", axis=0, tiled=True),
        lax.all_gather(w_up, "fsdp", axis=0, tiled=True),
        lax.all_gather(w_down, "fsdp", axis=1, tiled=True),
    )
    gain_one = full[0].astype(jnp.float32)
    gain_two = full[5].astype(jnp.float32)
    slots = tokens.shape[0]
    rows = tokens.shape[1]
    model = tokens.shape[2]
    flat = slots * rows
    x = tokens.astype(jnp.float32).reshape(flat, model)
    width = full[1].shape[1]
    heads = width // HD
    scale = HD ** (-0.5)
    cosine, sine = rope_angles(lax.axis_index("ctx") * rows, rows, HD)
    normed_one, rstd_one = layer_norm(x)
    h_one = (normed_one * gain_one).astype(jnp.bfloat16)
    query = rotate(
        matmul(h_one, full[1]).reshape(slots, rows, heads, HD), cosine, sine, 1.0
    ).astype(jnp.bfloat16)
    key_flat = (
        rotate(matmul(h_one, full[2]).reshape(slots, rows, heads, HD), cosine, sine, 1.0)
        .astype(jnp.bfloat16)
        .reshape(slots, rows, width)
    )
    value_flat = matmul(h_one, full[3]).astype(jnp.bfloat16).reshape(slots, rows, width)
    piece = (
        lax.all_gather(key_flat, "ctx", axis=1, tiled=True),
        lax.all_gather(value_flat, "ctx", axis=1, tiled=True),
    )
    best = jnp.full((slots, heads, rows), -1e30, jnp.float32)
    keys = piece[0].reshape(slots, -1, heads, HD)
    values = piece[1].reshape(slots, -1, heads, HD)
    scores = jnp.einsum("bqhd,bkhd->bhqk", query, keys, preferred_element_type=jnp.float32) * scale
    newbest = jnp.maximum(best, jnp.max(scores, axis=-1))
    weights = jnp.exp(scores - newbest[..., None])
    total = jnp.sum(weights, axis=-1)
    accum = jnp.einsum(
        "bhqk,bkhd->bhqd", weights.astype(jnp.bfloat16), values, preferred_element_type=jnp.float32
    )
    best, total, accum = (newbest, total, accum)
    log_total = best + jnp.log(total)
    attended = (
        (accum / total[..., None]).transpose(0, 2, 1, 3).reshape(flat, width).astype(jnp.bfloat16)
    )
    x_two = x + lax.psum(matmul(attended, full[4]).astype(jnp.bfloat16), "tp").astype(jnp.float32)
    normed_two, rstd_two = layer_norm(x_two)
    h_two = (normed_two * gain_two).astype(jnp.bfloat16)
    gate = matmul(h_two, full[6])
    up_part = matmul(h_two, full[7])
    activated, gelu_back = jax.vjp(partial(jax.nn.gelu, approximate=False), gate)
    hidden = (activated * up_part).astype(jnp.bfloat16)
    result = x_two + lax.psum(matmul(hidden, full[8]).astype(jnp.bfloat16), "tp").astype(
        jnp.float32
    )
    output = result.astype(jnp.bfloat16).reshape(slots, rows, model)
    grad_y = cotangent.astype(jnp.float32).reshape(flat, model)
    grad_low = grad_y.astype(jnp.bfloat16)
    grad_hidden = matmul(grad_low, full[8].T)
    grad_down = matmul(hidden.T, grad_low)
    grad_gate_act = gelu_back(grad_hidden * up_part)[0].astype(jnp.bfloat16)
    grad_up_act = (grad_hidden * activated).astype(jnp.bfloat16)
    grad_gate = matmul(h_two.T, grad_gate_act)
    grad_up = matmul(h_two.T, grad_up_act)
    grad_h_two = lax.psum(
        (matmul(grad_gate_act, full[6].T) + matmul(grad_up_act, full[7].T)).astype(jnp.bfloat16),
        "tp",
    ).astype(jnp.float32)
    grad_gain_ffn = jnp.sum(grad_h_two * normed_two, axis=0)
    grad_x_two = grad_y + norm_back(grad_h_two * gain_two, normed_two, rstd_two)
    branch_low = grad_x_two.astype(jnp.bfloat16)
    grad_out = matmul(attended.T, branch_low)
    grad_att = matmul(branch_low, full[4].T).astype(jnp.bfloat16)
    delta_rows = jnp.sum(
        (grad_att.astype(jnp.float32) * attended.astype(jnp.float32)).reshape(
            slots, rows, heads, HD
        ),
        axis=-1,
    )
    delta = delta_rows.transpose(0, 2, 1)
    grad_att_heads = grad_att.reshape(slots, rows, heads, HD)
    stats_all = (
        lax.all_gather(log_total.transpose(0, 2, 1), "ctx", axis=1, tiled=True),
        lax.all_gather(delta_rows, "ctx", axis=1, tiled=True),
    )
    own_keys = key_flat.reshape(slots, rows, heads, HD)
    own_values = value_flat.reshape(slots, rows, heads, HD)
    piece = (
        lax.all_gather(query, "ctx", axis=1, tiled=True),
        lax.all_gather(grad_att_heads, "ctx", axis=1, tiled=True),
    )
    queries = piece[0]
    grads_in = piece[1]
    lse_piece = stats_all[0].transpose(0, 2, 1)
    delta_piece = stats_all[1].transpose(0, 2, 1)
    scores = (
        jnp.einsum("bqhd,bkhd->bhqk", queries, own_keys, preferred_element_type=jnp.float32) * scale
    )
    probs = jnp.exp(scores - lse_piece[..., None])
    grad_probs = jnp.einsum(
        "bqhd,bkhd->bhqk", grads_in, own_values, preferred_element_type=jnp.float32
    )
    grad_scores = (probs * (grad_probs - delta_piece[..., None])).astype(jnp.bfloat16)
    grad_keys_acc = (
        jnp.einsum("bhqk,bqhd->bkhd", grad_scores, queries, preferred_element_type=jnp.float32)
        * scale
    )
    grad_values_acc = jnp.einsum(
        "bhqk,bqhd->bkhd", probs.astype(jnp.bfloat16), grads_in, preferred_element_type=jnp.float32
    )
    piece = (
        lax.all_gather(key_flat, "ctx", axis=1, tiled=True),
        lax.all_gather(value_flat, "ctx", axis=1, tiled=True),
    )
    keys = piece[0].reshape(slots, -1, heads, HD)
    values = piece[1].reshape(slots, -1, heads, HD)
    scores = jnp.einsum("bqhd,bkhd->bhqk", query, keys, preferred_element_type=jnp.float32) * scale
    probs = jnp.exp(scores - log_total[..., None])
    grad_probs = jnp.einsum(
        "bqhd,bkhd->bhqk", grad_att_heads, values, preferred_element_type=jnp.float32
    )
    grad_scores = (probs * (grad_probs - delta[..., None])).astype(jnp.bfloat16)
    probs, grad_scores = (probs, grad_scores)
    grad_query_rot = (
        jnp.einsum("bhqk,bkhd->bqhd", grad_scores, keys, preferred_element_type=jnp.float32) * scale
    )
    grad_query_raw = (
        rotate(grad_query_rot, cosine, sine, -1.0).reshape(flat, width).astype(jnp.bfloat16)
    )
    grad_key_raw = (
        rotate(grad_keys_acc, cosine, sine, -1.0).reshape(flat, width).astype(jnp.bfloat16)
    )
    grad_value_raw = grad_values_acc.reshape(flat, width).astype(jnp.bfloat16)
    grad_query = matmul(h_one.T, grad_query_raw)
    grad_key = matmul(h_one.T, grad_key_raw)
    grad_value = matmul(h_one.T, grad_value_raw)
    grad_h_one = lax.psum(
        (
            matmul(grad_query_raw, full[1].T)
            + matmul(grad_key_raw, full[2].T)
            + matmul(grad_value_raw, full[3].T)
        ).astype(jnp.bfloat16),
        "tp",
    ).astype(jnp.float32)
    grad_gain_attn = jnp.sum(grad_h_one * normed_one, axis=0)
    grad_tokens = (grad_x_two + norm_back(grad_h_one * gain_one, normed_one, rstd_one)).reshape(
        slots, rows, model
    )
    pieces = (
        lax.psum_scatter(
            grad_gain_attn.astype(jnp.bfloat16), "fsdp", scatter_dimension=0, tiled=True
        ).astype(jnp.float32),
        lax.psum_scatter(
            grad_query.astype(jnp.bfloat16), "fsdp", scatter_dimension=0, tiled=True
        ).astype(jnp.float32),
        lax.psum_scatter(
            grad_key.astype(jnp.bfloat16), "fsdp", scatter_dimension=0, tiled=True
        ).astype(jnp.float32),
        lax.psum_scatter(
            grad_value.astype(jnp.bfloat16), "fsdp", scatter_dimension=0, tiled=True
        ).astype(jnp.float32),
        lax.psum_scatter(
            grad_out.astype(jnp.bfloat16), "fsdp", scatter_dimension=1, tiled=True
        ).astype(jnp.float32),
        lax.psum_scatter(
            grad_gain_ffn.astype(jnp.bfloat16), "fsdp", scatter_dimension=0, tiled=True
        ).astype(jnp.float32),
        lax.psum_scatter(
            grad_gate.astype(jnp.bfloat16), "fsdp", scatter_dimension=0, tiled=True
        ).astype(jnp.float32),
        lax.psum_scatter(
            grad_up.astype(jnp.bfloat16), "fsdp", scatter_dimension=0, tiled=True
        ).astype(jnp.float32),
        lax.psum_scatter(
            grad_down.astype(jnp.bfloat16), "fsdp", scatter_dimension=1, tiled=True
        ).astype(jnp.float32),
    )
    owned = (
        lax.psum(pieces[0].astype(jnp.bfloat16), "ctx").astype(jnp.float32),
        lax.psum(pieces[1].astype(jnp.bfloat16), "ctx").astype(jnp.float32),
        lax.psum(pieces[2].astype(jnp.bfloat16), "ctx").astype(jnp.float32),
        lax.psum(pieces[3].astype(jnp.bfloat16), "ctx").astype(jnp.float32),
        lax.psum(pieces[4].astype(jnp.bfloat16), "ctx").astype(jnp.float32),
        lax.psum(pieces[5].astype(jnp.bfloat16), "ctx").astype(jnp.float32),
        lax.psum(pieces[6].astype(jnp.bfloat16), "ctx").astype(jnp.float32),
        lax.psum(pieces[7].astype(jnp.bfloat16), "ctx").astype(jnp.float32),
        lax.psum(pieces[8].astype(jnp.bfloat16), "ctx").astype(jnp.float32),
    )
    return (
        output,
        grad_tokens,
        owned[0],
        owned[1],
        owned[2],
        owned[3],
        owned[4],
        owned[5],
        owned[6],
        owned[7],
        owned[8],
    )


swapped = ((0, 1), (1, 0))


def gather_rows(shard, after=None):
    if after is not None:
        shard, _ = lax.optimization_barrier((shard, after))
    count = lax.axis_size("fsdp")
    me = lax.axis_index("fsdp")
    whole = jnp.zeros((count,) + shard.shape, shard.dtype)
    whole = lax.dynamic_update_index_in_dim(whole, shard, me, 0)
    for step in range(1, count):
        came = lax.ppermute(shard, "fsdp", [(i, i ^ step) for i in range(count)])
        whole = lax.dynamic_update_index_in_dim(whole, came, me ^ step, 0)
    return whole.reshape((-1,) + shard.shape[1:])


def scatter_blocks(blocks):
    count = lax.axis_size("fsdp")
    me = lax.axis_index("fsdp")
    total = lax.dynamic_index_in_dim(blocks, me, 0, keepdims=False).astype(jnp.float32)
    for step in range(1, count):
        give = lax.dynamic_index_in_dim(blocks, me ^ step, 0, keepdims=False)
        came = lax.ppermute(give, "fsdp", [(i, i ^ step) for i in range(count)])
        total = total + came.astype(jnp.float32)
    low = total.astype(blocks.dtype)
    other = lax.ppermute(low, "ctx", swapped)
    return low.astype(jnp.float32) + other.astype(jnp.float32)


def scatter_rows(grad):
    count = lax.axis_size("fsdp")
    return scatter_blocks(grad.astype(jnp.bfloat16).reshape(count, -1, grad.shape[1]))


def sum_tp(part):
    part = part.astype(jnp.bfloat16)
    other = lax.ppermute(part, "tp", swapped)
    return part.astype(jnp.float32) + other.astype(jnp.float32)


def take_sequence(blocks):
    c = lax.axis_index("ctx")
    own = lax.dynamic_index_in_dim(blocks, c, 0, keepdims=False)
    give = lax.dynamic_index_in_dim(blocks, 1 - c, 0, keepdims=False)
    return jnp.concatenate([own, lax.ppermute(give, "ctx", swapped)], axis=0)


def give_back(own, came):
    c = lax.axis_index("ctx")
    return jnp.where(c == 0, jnp.stack([own, came]), jnp.stack([came, own]))


def dot(a, b, over):
    return lax.dot_general(a, b, (over, ((), ())), preferred_element_type=jnp.float32)


def turn(u):
    lane = lax.broadcasted_iota(jnp.int32, u.shape, 1)
    return jnp.where(lane % HD < HD // 2, -pltpu.roll(u, 96, 1), pltpu.roll(u, 32, 1))


def attend_kernel(h_ref, w_ref, cos_ref, sin_ref, q_ref, k_ref, v_ref, o_ref, lse_ref, *, tile):
    rows = h_ref.shape[0]
    raw = jnp.dot(h_ref[...], w_ref[...], preferred_element_type=jnp.float32)
    cosine, sine = cos_ref[...], sin_ref[...]
    q_raw, k_raw = raw[:, :128], raw[:, 128:256]
    q_ref[...] = (q_raw * cosine + turn(q_raw) * sine).astype(jnp.bfloat16)
    k_ref[...] = (k_raw * cosine + turn(k_raw) * sine).astype(jnp.bfloat16)
    v = raw[:, 256:]
    v_ref[...] = v.astype(jnp.bfloat16)
    v_turned = v.T.astype(jnp.bfloat16)
    k = k_ref[...]
    lane = lax.broadcasted_iota(jnp.int32, (tile, 128), 1)
    for start in range(0, rows, tile):
        at = slice(start, start + tile)
        q = q_ref[at, :] * jnp.bfloat16(HD ** (-0.5))
        outs = []
        for head in range(2):
            mine = (lane // HD) == head
            qm = jnp.where(mine, q, jnp.zeros_like(q))
            s = dot(k, qm, ((1,), (1,)))
            top = jnp.max(s, axis=0, keepdims=True)
            e = jnp.exp(s - top)
            total = jnp.sum(e, axis=0, keepdims=True)
            lse_ref[0, head : head + 1, at] = top + jnp.log(total)
            vh = v_turned[head * HD : (head + 1) * HD]
            outs.append(dot(vh, e.astype(jnp.bfloat16), ((1,), (0,))) / total)
        o_ref[at, :] = jnp.concatenate(outs, axis=0).T.astype(jnp.bfloat16)


def attend_back_kernel(
    q_ref, k_ref, v_ref, o_ref, do_ref, lse_ref, cos_ref, sin_ref, out_ref, dk_ref, dv_ref, *, tile
):
    rows = q_ref.shape[0]
    k, v = k_ref[...], v_ref[...]
    k_turned = k.astype(jnp.float32).T.astype(jnp.bfloat16)
    lane = lax.broadcasted_iota(jnp.int32, (tile, 128), 1)
    dk_ref[...] = jnp.zeros_like(dk_ref)
    dv_ref[...] = jnp.zeros_like(dv_ref)
    for start in range(0, rows, tile):
        at = slice(start, start + tile)
        q = q_ref[at, :] * jnp.bfloat16(HD ** (-0.5))
        do = do_ref[at, :]
        prod = (do.astype(jnp.float32) * o_ref[at, :].astype(jnp.float32)).T
        outs = []
        for head in range(2):
            mine = (lane // HD) == head
            qm = jnp.where(mine, q, jnp.zeros_like(q))
            dm = jnp.where(mine, do, jnp.zeros_like(do))
            delta = jnp.sum(prod[head * HD : (head + 1) * HD], axis=0, keepdims=True)
            p = jnp.exp(dot(k, qm, ((1,), (1,))) - lse_ref[0, head : head + 1, at])
            ds = (p * (dot(v, dm, ((1,), (1,))) - delta)).astype(jnp.bfloat16)
            dv_ref[...] += dot(p.astype(jnp.bfloat16), dm, ((1,), (0,)))
            dk_ref[...] += dot(ds, qm, ((1,), (0,)))
            outs.append(dot(k_turned[head * HD : (head + 1) * HD], ds, ((1,), (0,))))
        dq = jnp.concatenate(outs, axis=0).T * (HD ** (-0.5))
        dq = dq * cos_ref[at, :] - turn(dq) * sin_ref[at, :]
        out_ref[at, :128] = dq.astype(jnp.bfloat16)
    dk = dk_ref[...]
    out_ref[:, 128:256] = (dk * cos_ref[...] - turn(dk) * sin_ref[...]).astype(jnp.bfloat16)
    out_ref[:, 256:] = dv_ref[...].astype(jnp.bfloat16)


def attend(h_one, w_pairs, cosine, sine):
    rows, model = h_one.shape
    pairs = w_pairs.shape[1] // 384
    width = pairs * 128
    column = pl.BlockSpec((rows, 128), lambda i: (0, i))
    table = pl.BlockSpec((rows, 128), lambda i: (0, 0))
    low = jax.ShapeDtypeStruct((rows, width), jnp.bfloat16)
    return pl.pallas_call(
        partial(attend_kernel, tile=min(512, rows)),
        grid=(pairs,),
        in_specs=[
            pl.BlockSpec((rows, model), lambda i: (0, 0)),
            pl.BlockSpec((model, 384), lambda i: (0, i)),
            table,
            table,
        ],
        out_specs=[column] * 4 + [pl.BlockSpec((1, 2, rows), lambda i: (i, 0, 0))],
        out_shape=[low] * 4 + [jax.ShapeDtypeStruct((pairs, 2, rows), jnp.float32)],
        compiler_params=pltpu.CompilerParams(vmem_limit_bytes=44 << 20),
        cost_estimate=pl.CostEstimate(
            flops=16 * 10**9, bytes_accessed=10**7, transcendentals=pairs * 2 * rows * rows
        ),
        name="attend",
    )(h_one, w_pairs, cosine, sine)


def attend_back(q, k, v, o, do, lse, cosine, sine):
    rows, width = q.shape
    pairs = width // 128
    column = pl.BlockSpec((rows, 128), lambda i: (0, i))
    table = pl.BlockSpec((rows, 128), lambda i: (0, 0))
    return pl.pallas_call(
        partial(attend_back_kernel, tile=min(512, rows)),
        grid=(pairs,),
        in_specs=[column] * 5 + [pl.BlockSpec((1, 2, rows), lambda i: (i, 0, 0)), table, table],
        out_specs=pl.BlockSpec((rows, 384), lambda i: (0, i)),
        out_shape=jax.ShapeDtypeStruct((rows, 3 * width), jnp.bfloat16),
        scratch_shapes=[pltpu.VMEM((rows, 128), jnp.float32)] * 2,
        compiler_params=pltpu.CompilerParams(vmem_limit_bytes=44 << 20),
        cost_estimate=pl.CostEstimate(
            flops=30 * 10**9, bytes_accessed=10**7, transcendentals=pairs * 2 * rows * rows
        ),
        name="attend_back",
    )(q, k, v, o, do, lse, cosine, sine)


def rope_tables(rows):
    angle = np.arange(2 * rows, dtype=np.float32)[:, None] * (
        np.float32(1.0)
        / np.float32(rope_base) ** (np.arange(0, HD, 2, dtype=np.float32) / np.float32(HD))
    )[None, :].astype(np.float32)
    tables = []
    for values in (np.cos(angle), np.sin(angle)):
        whole = jnp.asarray(np.tile(values.astype(np.float32), (1, 4)))
        flipped = jnp.concatenate([whole[rows:], whole[:rows]], axis=0)
        tables.append(jnp.where(lax.axis_index("ctx") == 0, whole, flipped))
    return tables


def on_device(
    tokens, gain_attn, w_query, w_key, w_value, w_out, gain_ffn, w_gate, w_up, w_down, cotangent
):
    slots, rows, model = tokens.shape
    part = w_query.shape[0]
    width = w_query.shape[1]
    pairs = width // 128
    units = w_gate.shape[1]
    packed = jnp.stack(
        [w.reshape(part, pairs, 128) for w in (w_query, w_key, w_value)], axis=2
    ).reshape(part, 3 * width)
    gains = lax.all_gather(jnp.stack([gain_attn, gain_ffn]), "fsdp", axis=1, tiled=True)
    gain_one, gain_two = gains[0].astype(jnp.float32), gains[1].astype(jnp.float32)
    x = take_sequence(tokens).astype(jnp.float32)
    qkv_w = gather_rows(packed)
    out_w = gather_rows(w_out.T, qkv_w)
    ffn_w = gather_rows(jnp.concatenate([w_gate, w_up], axis=1), qkv_w)
    down_w = gather_rows(w_down.T, qkv_w)
    cotangent, _ = lax.optimization_barrier((cotangent, qkv_w))
    grad_low = take_sequence(cotangent)
    grad_y = grad_low.astype(jnp.float32)
    cosine, sine = rope_tables(rows)

    normed_one, rstd_one = layer_norm(x)
    h_one = (normed_one * gain_one).astype(jnp.bfloat16)
    q, k, v, attended, lse = attend(h_one, qkv_w, cosine, sine)
    x_two = x + sum_tp(dot(attended, out_w, ((1,), (1,))))
    normed_two, rstd_two = layer_norm(x_two)
    h_two = (normed_two * gain_two).astype(jnp.bfloat16)
    both = matmul(h_two, ffn_w)
    gate, up_part = both[:, :units], both[:, units:]
    activated, gelu_back = jax.vjp(partial(jax.nn.gelu, approximate=False), gate)
    hidden = (activated * up_part).astype(jnp.bfloat16)
    output = (x_two + sum_tp(dot(hidden, down_w, ((1,), (1,))))).astype(jnp.bfloat16)
    output = give_back(output[:rows], lax.ppermute(output[rows:], "ctx", swapped))

    grad_hidden = matmul(grad_low, down_w)
    grad_both = jnp.concatenate(
        [
            gelu_back(grad_hidden * up_part)[0].astype(jnp.bfloat16),
            (grad_hidden * activated).astype(jnp.bfloat16),
        ],
        axis=1,
    )
    grad_h_two = sum_tp(dot(grad_both, ffn_w, ((1,), (1,))))
    own_ffn = scatter_rows(dot(h_two, grad_both, ((0,), (0,))))
    own_down = scatter_rows(dot(grad_low, hidden, ((0,), (0,))))
    grad_gain_ffn = jnp.sum(grad_h_two * normed_two, axis=0)
    grad_x_two = grad_y + norm_back(grad_h_two * gain_two, normed_two, rstd_two)
    branch_low = grad_x_two.astype(jnp.bfloat16)
    own_out = scatter_rows(dot(branch_low, attended, ((0,), (0,))))
    grad_att = matmul(branch_low, out_w).astype(jnp.bfloat16)
    grad_qkv = attend_back(q, k, v, attended, grad_att, lse, cosine, sine)
    grad_h_one = sum_tp(dot(grad_qkv, qkv_w, ((1,), (1,))))
    own_qkv = scatter_rows(dot(h_one, grad_qkv, ((0,), (0,))))
    grad_gain_attn = jnp.sum(grad_h_one * normed_one, axis=0)
    grad_x = grad_x_two + norm_back(grad_h_one * gain_one, normed_one, rstd_one)
    came = lax.ppermute(grad_x[rows:].astype(jnp.bfloat16), "ctx", swapped).astype(jnp.float32)
    grad_tokens = give_back(grad_x[:rows], came)
    own_gains = scatter_blocks(
        jnp.stack([grad_gain_attn, grad_gain_ffn]).reshape(2, -1, part).transpose(1, 0, 2)
    )
    own_qkv = own_qkv.reshape(part, pairs, 3, 128)
    return (
        output,
        grad_tokens,
        own_gains[0],
        own_qkv[:, :, 0].reshape(part, width),
        own_qkv[:, :, 1].reshape(part, width),
        own_qkv[:, :, 2].reshape(part, width),
        own_out.T,
        own_gains[1],
        own_ffn[:, :units],
        own_ffn[:, units:],
        own_down.T,
    )


def solution(mesh):
    whole = mesh.shape["ctx"] == 2 and mesh.shape["tp"] == 2
    step = on_device if whole and mesh.shape["fsdp"] == 8 else on_device_blocks
    placed = (
        P(None, ("fsdp", "ctx"), None),
        P("fsdp"),
        P("fsdp", "tp"),
        P("fsdp", "tp"),
        P("fsdp", "tp"),
        P("tp", "fsdp"),
        P("fsdp"),
        P("fsdp", "tp"),
        P("fsdp", "tp"),
        P("tp", "fsdp"),
        P(None, ("fsdp", "ctx"), None),
    )
    return jax.shard_map(
        step,
        mesh=mesh,
        in_specs=placed,
        out_specs=(
            P(None, ("fsdp", "ctx"), None),
            P(None, ("fsdp", "ctx"), None),
            P("fsdp"),
            P("fsdp", "tp"),
            P("fsdp", "tp"),
            P("fsdp", "tp"),
            P("tp", "fsdp"),
            P("fsdp"),
            P("fsdp", "tp"),
            P("fsdp", "tp"),
            P("tp", "fsdp"),
        ),
        check_vma=False,
    )
```

```python
from functools import partial

import jax
import jax.numpy as jnp
import numpy as np
from jax import lax
from jax.experimental import pallas as pl
from jax.experimental.pallas import tpu as pltpu
from jax.sharding import PartitionSpec as P

HD = 64


eps_norm = 1e-05
rope_base = 160000.0


def layer_norm(x):
    mean = jnp.mean(x, axis=-1, keepdims=True)
    centred = x - mean
    var = jnp.mean(centred * centred, axis=-1, keepdims=True)
    rstd = lax.rsqrt(var + eps_norm)
    return (centred * rstd, rstd)


def norm_back(grad_normed, normed, rstd):
    first = jnp.mean(grad_normed, axis=-1, keepdims=True)
    second = jnp.mean(grad_normed * normed, axis=-1, keepdims=True)
    return rstd * (grad_normed - first - normed * second)


def rope_angles(first, count, width):
    position = (first + jnp.arange(count, dtype=jnp.int32)).astype(jnp.float32)
    inverse = 1.0 / rope_base ** (
        jnp.arange(0, width, 2, dtype=jnp.int32).astype(jnp.float32) / width
    )
    angle = position[:, None] * inverse[None, :]
    angle = jnp.concatenate([angle, angle], axis=-1)
    return (jnp.cos(angle), jnp.sin(angle))


def rotate(heads, cosine, sine, sign):
    half = heads.shape[-1] // 2
    turned = jnp.concatenate([-heads[..., half:], heads[..., :half]], axis=-1)
    return heads * cosine[:, None, :] + sign * turned * sine[:, None, :]


def matmul(a, b):
    return jnp.dot(a, b, preferred_element_type=jnp.float32)


def on_device_blocks(
    tokens, gain_attn, w_query, w_key, w_value, w_out, gain_ffn, w_gate, w_up, w_down, cotangent
):
    full = (
        lax.all_gather(gain_attn, "fsdp", axis=0, tiled=True),
        lax.all_gather(w_query, "fsdp", axis=0, tiled=True),
        lax.all_gather(w_key, "fsdp", axis=0, tiled=True),
        lax.all_gather(w_value, "fsdp", axis=0, tiled=True),
        lax.all_gather(w_out, "fsdp", axis=1, tiled=True),
        lax.all_gather(gain_ffn, "fsdp", axis=0, tiled=True),
        lax.all_gather(w_gate, "fsdp", axis=0, tiled=True),
        lax.all_gather(w_up, "fsdp", axis=0, tiled=True),
        lax.all_gather(w_down, "fsdp", axis=1, tiled=True),
    )
    gain_one = full[0].astype(jnp.float32)
    gain_two = full[5].astype(jnp.float32)
    slots = tokens.shape[0]
    rows = tokens.shape[1]
    model = tokens.shape[2]
    flat = slots * rows
    x = tokens.astype(jnp.float32).reshape(flat, model)
    width = full[1].shape[1]
    heads = width // HD
    scale = HD ** (-0.5)
    cosine, sine = rope_angles(lax.axis_index("ctx") * rows, rows, HD)
    normed_one, rstd_one = layer_norm(x)
    h_one = (normed_one * gain_one).astype(jnp.bfloat16)
    query = rotate(
        matmul(h_one, full[1]).reshape(slots, rows, heads, HD), cosine, sine, 1.0
    ).astype(jnp.bfloat16)
    key_flat = (
        rotate(matmul(h_one, full[2]).reshape(slots, rows, heads, HD), cosine, sine, 1.0)
        .astype(jnp.bfloat16)
        .reshape(slots, rows, width)
    )
    value_flat = matmul(h_one, full[3]).astype(jnp.bfloat16).reshape(slots, rows, width)
    piece = (
        lax.all_gather(key_flat, "ctx", axis=1, tiled=True),
        lax.all_gather(value_flat, "ctx", axis=1, tiled=True),
    )
    best = jnp.full((slots, heads, rows), -1e30, jnp.float32)
    keys = piece[0].reshape(slots, -1, heads, HD)
    values = piece[1].reshape(slots, -1, heads, HD)
    scores = jnp.einsum("bqhd,bkhd->bhqk", query, keys, preferred_element_type=jnp.float32) * scale
    newbest = jnp.maximum(best, jnp.max(scores, axis=-1))
    weights = jnp.exp(scores - newbest[..., None])
    total = jnp.sum(weights, axis=-1)
    accum = jnp.einsum(
        "bhqk,bkhd->bhqd", weights.astype(jnp.bfloat16), values, preferred_element_type=jnp.float32
    )
    best, total, accum = (newbest, total, accum)
    log_total = best + jnp.log(total)
    attended = (
        (accum / total[..., None]).transpose(0, 2, 1, 3).reshape(flat, width).astype(jnp.bfloat16)
    )
    x_two = x + lax.psum(matmul(attended, full[4]).astype(jnp.bfloat16), "tp").astype(jnp.float32)
    normed_two, rstd_two = layer_norm(x_two)
    h_two = (normed_two * gain_two).astype(jnp.bfloat16)
    gate = matmul(h_two, full[6])
    up_part = matmul(h_two, full[7])
    activated, gelu_back = jax.vjp(partial(jax.nn.gelu, approximate=False), gate)
    hidden = (activated * up_part).astype(jnp.bfloat16)
    result = x_two + lax.psum(matmul(hidden, full[8]).astype(jnp.bfloat16), "tp").astype(
        jnp.float32
    )
    output = result.astype(jnp.bfloat16).reshape(slots, rows, model)
    grad_y = cotangent.astype(jnp.float32).reshape(flat, model)
    grad_low = grad_y.astype(jnp.bfloat16)
    grad_hidden = matmul(grad_low, full[8].T)
    grad_down = matmul(hidden.T, grad_low)
    grad_gate_act = gelu_back(grad_hidden * up_part)[0].astype(jnp.bfloat16)
    grad_up_act = (grad_hidden * activated).astype(jnp.bfloat16)
    grad_gate = matmul(h_two.T, grad_gate_act)
    grad_up = matmul(h_two.T, grad_up_act)
    grad_h_two = lax.psum(
        (matmul(grad_gate_act, full[6].T) + matmul(grad_up_act, full[7].T)).astype(jnp.bfloat16),
        "tp",
    ).astype(jnp.float32)
    grad_gain_ffn = jnp.sum(grad_h_two * normed_two, axis=0)
    grad_x_two = grad_y + norm_back(grad_h_two * gain_two, normed_two, rstd_two)
    branch_low = grad_x_two.astype(jnp.bfloat16)
    grad_out = matmul(attended.T, branch_low)
    grad_att = matmul(branch_low, full[4].T).astype(jnp.bfloat16)
    delta_rows = jnp.sum(
        (grad_att.astype(jnp.float32) * attended.astype(jnp.float32)).reshape(
            slots, rows, heads, HD
        ),
        axis=-1,
    )
    delta = delta_rows.transpose(0, 2, 1)
    grad_att_heads = grad_att.reshape(slots, rows, heads, HD)
    stats_all = (
        lax.all_gather(log_total.transpose(0, 2, 1), "ctx", axis=1, tiled=True),
        lax.all_gather(delta_rows, "ctx", axis=1, tiled=True),
    )
    own_keys = key_flat.reshape(slots, rows, heads, HD)
    own_values = value_flat.reshape(slots, rows, heads, HD)
    piece = (
        lax.all_gather(query, "ctx", axis=1, tiled=True),
        lax.all_gather(grad_att_heads, "ctx", axis=1, tiled=True),
    )
    queries = piece[0]
    grads_in = piece[1]
    lse_piece = stats_all[0].transpose(0, 2, 1)
    delta_piece = stats_all[1].transpose(0, 2, 1)
    scores = (
        jnp.einsum("bqhd,bkhd->bhqk", queries, own_keys, preferred_element_type=jnp.float32) * scale
    )
    probs = jnp.exp(scores - lse_piece[..., None])
    grad_probs = jnp.einsum(
        "bqhd,bkhd->bhqk", grads_in, own_values, preferred_element_type=jnp.float32
    )
    grad_scores = (probs * (grad_probs - delta_piece[..., None])).astype(jnp.bfloat16)
    grad_keys_acc = (
        jnp.einsum("bhqk,bqhd->bkhd", grad_scores, queries, preferred_element_type=jnp.float32)
        * scale
    )
    grad_values_acc = jnp.einsum(
        "bhqk,bqhd->bkhd", probs.astype(jnp.bfloat16), grads_in, preferred_element_type=jnp.float32
    )
    piece = (
        lax.all_gather(key_flat, "ctx", axis=1, tiled=True),
        lax.all_gather(value_flat, "ctx", axis=1, tiled=True),
    )
    keys = piece[0].reshape(slots, -1, heads, HD)
    values = piece[1].reshape(slots, -1, heads, HD)
    scores = jnp.einsum("bqhd,bkhd->bhqk", query, keys, preferred_element_type=jnp.float32) * scale
    probs = jnp.exp(scores - log_total[..., None])
    grad_probs = jnp.einsum(
        "bqhd,bkhd->bhqk", grad_att_heads, values, preferred_element_type=jnp.float32
    )
    grad_scores = (probs * (grad_probs - delta[..., None])).astype(jnp.bfloat16)
    probs, grad_scores = (probs, grad_scores)
    grad_query_rot = (
        jnp.einsum("bhqk,bkhd->bqhd", grad_scores, keys, preferred_element_type=jnp.float32) * scale
    )
    grad_query_raw = (
        rotate(grad_query_rot, cosine, sine, -1.0).reshape(flat, width).astype(jnp.bfloat16)
    )
    grad_key_raw = (
        rotate(grad_keys_acc, cosine, sine, -1.0).reshape(flat, width).astype(jnp.bfloat16)
    )
    grad_value_raw = grad_values_acc.reshape(flat, width).astype(jnp.bfloat16)
    grad_query = matmul(h_one.T, grad_query_raw)
    grad_key = matmul(h_one.T, grad_key_raw)
    grad_value = matmul(h_one.T, grad_value_raw)
    grad_h_one = lax.psum(
        (
            matmul(grad_query_raw, full[1].T)
            + matmul(grad_key_raw, full[2].T)
            + matmul(grad_value_raw, full[3].T)
        ).astype(jnp.bfloat16),
        "tp",
    ).astype(jnp.float32)
    grad_gain_attn = jnp.sum(grad_h_one * normed_one, axis=0)
    grad_tokens = (grad_x_two + norm_back(grad_h_one * gain_one, normed_one, rstd_one)).reshape(
        slots, rows, model
    )
    pieces = (
        lax.psum_scatter(
            grad_gain_attn.astype(jnp.bfloat16), "fsdp", scatter_dimension=0, tiled=True
        ).astype(jnp.float32),
        lax.psum_scatter(
            grad_query.astype(jnp.bfloat16), "fsdp", scatter_dimension=0, tiled=True
        ).astype(jnp.float32),
        lax.psum_scatter(
            grad_key.astype(jnp.bfloat16), "fsdp", scatter_dimension=0, tiled=True
        ).astype(jnp.float32),
        lax.psum_scatter(
            grad_value.astype(jnp.bfloat16), "fsdp", scatter_dimension=0, tiled=True
        ).astype(jnp.float32),
        lax.psum_scatter(
            grad_out.astype(jnp.bfloat16), "fsdp", scatter_dimension=1, tiled=True
        ).astype(jnp.float32),
        lax.psum_scatter(
            grad_gain_ffn.astype(jnp.bfloat16), "fsdp", scatter_dimension=0, tiled=True
        ).astype(jnp.float32),
        lax.psum_scatter(
            grad_gate.astype(jnp.bfloat16), "fsdp", scatter_dimension=0, tiled=True
        ).astype(jnp.float32),
        lax.psum_scatter(
            grad_up.astype(jnp.bfloat16), "fsdp", scatter_dimension=0, tiled=True
        ).astype(jnp.float32),
        lax.psum_scatter(
            grad_down.astype(jnp.bfloat16), "fsdp", scatter_dimension=1, tiled=True
        ).astype(jnp.float32),
    )
    owned = (
        lax.psum(pieces[0].astype(jnp.bfloat16), "ctx").astype(jnp.float32),
        lax.psum(pieces[1].astype(jnp.bfloat16), "ctx").astype(jnp.float32),
        lax.psum(pieces[2].astype(jnp.bfloat16), "ctx").astype(jnp.float32),
        lax.psum(pieces[3].astype(jnp.bfloat16), "ctx").astype(jnp.float32),
        lax.psum(pieces[4].astype(jnp.bfloat16), "ctx").astype(jnp.float32),
        lax.psum(pieces[5].astype(jnp.bfloat16), "ctx").astype(jnp.float32),
        lax.psum(pieces[6].astype(jnp.bfloat16), "ctx").astype(jnp.float32),
        lax.psum(pieces[7].astype(jnp.bfloat16), "ctx").astype(jnp.float32),
        lax.psum(pieces[8].astype(jnp.bfloat16), "ctx").astype(jnp.float32),
    )
    return (
        output,
        grad_tokens,
        owned[0],
        owned[1],
        owned[2],
        owned[3],
        owned[4],
        owned[5],
        owned[6],
        owned[7],
        owned[8],
    )


swapped = ((0, 1), (1, 0))


MESH = pl.DeviceIdType.MESH


def greet(with_ctx):
    count = lax.axis_size("fsdp")
    me = lax.axis_index("fsdp")
    barrier = pltpu.get_barrier_semaphore()
    for step in range(1, count):
        there = lax.rem(me + step, count)
        pl.semaphore_signal(barrier, inc=1, device_id={"fsdp": there}, device_id_type=MESH)
    if with_ctx:
        there = 1 - lax.axis_index("ctx")
        pl.semaphore_signal(barrier, inc=1, device_id={"ctx": there}, device_id_type=MESH)
    pl.semaphore_wait(barrier, count - 1 + int(with_ctx))


def gather_copies(src, dst, send, recv, local):
    count = lax.axis_size("fsdp")
    me = lax.axis_index("fsdp")
    copies = [pltpu.make_async_copy(src, dst.at[me], local)]
    for step in range(1, count):
        copies.append(
            pltpu.make_async_remote_copy(
                src_ref=src,
                dst_ref=dst.at[me],
                send_sem=send.at[step - 1],
                recv_sem=recv.at[step - 1],
                device_id={"fsdp": lax.rem(me + step, count)},
                device_id_type=MESH,
            )
        )
    return copies


def scatter_copies(src, slots, send, recv, local):
    count = lax.axis_size("fsdp")
    me = lax.axis_index("fsdp")
    copies = [pltpu.make_async_copy(src.at[me], slots.at[0], local)]
    for step in range(1, count):
        there = lax.rem(me + step, count)
        copies.append(
            pltpu.make_async_remote_copy(
                src_ref=src.at[there],
                dst_ref=slots.at[step],
                send_sem=send.at[step - 1],
                recv_sem=recv.at[step - 1],
                device_id={"fsdp": there},
                device_id_type=MESH,
            )
        )
    return copies


def add_up(slots, low, other, out, send, recv):
    total = slots[0].astype(jnp.float32)
    for step in range(1, slots.shape[0]):
        total += slots[step].astype(jnp.float32)
    low[...] = total.astype(low.dtype)
    copy = pltpu.make_async_remote_copy(
        src_ref=low,
        dst_ref=other,
        send_sem=send,
        recv_sem=recv,
        device_id={"ctx": 1 - lax.axis_index("ctx")},
        device_id_type=MESH,
    )
    copy.start()
    return copy


def finish_sums(groups, ctx_send, ctx_recv):
    later = []
    for n, (slots, low, other, out) in enumerate(groups):
        later.append(add_up(slots, low, other, out, ctx_send.at[n], ctx_recv.at[n]))
    for copy, (slots, low, other, out) in zip(later, groups):
        copy.wait()
        out[...] = low[...].astype(jnp.float32) + other[...].astype(jnp.float32)


def semaphores(arrays, count):
    return [
        pltpu.SemaphoreType.DMA((arrays, count - 1)),
        pltpu.SemaphoreType.DMA((arrays, count - 1)),
        pltpu.SemaphoreType.DMA((arrays,)),
    ]


def gather_kernel(*refs):
    many = (len(refs) - 3) // 2
    send, recv, local = refs[-3:]
    greet(False)
    copies = []
    for n in range(many):
        copies += gather_copies(refs[n], refs[many + n], send.at[n], recv.at[n], local.at[n])
    for copy in copies:
        copy.start()
    for copy in copies:
        copy.wait()


def gather(*shards):
    count = lax.axis_size("fsdp")
    return pl.pallas_call(
        gather_kernel,
        in_specs=[pl.BlockSpec(memory_space=pl.ANY)] * len(shards),
        out_specs=[pl.BlockSpec(memory_space=pl.ANY)] * len(shards),
        out_shape=[jax.ShapeDtypeStruct((count,) + s.shape, s.dtype) for s in shards],
        scratch_shapes=semaphores(len(shards), count),
        compiler_params=pltpu.CompilerParams(collective_id=0, has_side_effects=True),
        name="gather",
    )(*shards)


def sums_scratch(blocks):
    shapes = []
    for b in blocks:
        shapes += [pltpu.VMEM(b.shape, b.dtype)] + [pltpu.VMEM(b.shape[1:], b.dtype)] * 2
    many = len(blocks)
    return (
        shapes
        + semaphores(many, blocks[0].shape[0])
        + [pltpu.SemaphoreType.DMA((many,)), pltpu.SemaphoreType.DMA((many,))]
    )


def sums_parts(srcs, outs, scratch):
    many = len(srcs)
    send, recv, local, ctx_send, ctx_recv = scratch[3 * many :]
    copies, groups = [], []
    for n in range(many):
        slots, low, other = scratch[3 * n : 3 * n + 3]
        copies += scatter_copies(srcs[n], slots, send.at[n], recv.at[n], local.at[n])
        groups.append((slots, low, other, outs[n]))
    return copies, groups, ctx_send, ctx_recv


def scatter_kernel(*refs, many):
    greet(True)
    copies, groups, ctx_send, ctx_recv = sums_parts(
        refs[:many], refs[many : 2 * many], refs[2 * many :]
    )
    for copy in copies:
        copy.start()
    for copy in copies:
        copy.wait()
    finish_sums(groups, ctx_send, ctx_recv)


def scatter(*blocks):
    return pl.pallas_call(
        partial(scatter_kernel, many=len(blocks)),
        in_specs=[pl.BlockSpec(memory_space=pl.ANY)] * len(blocks),
        out_specs=[pl.BlockSpec(memory_space=pltpu.VMEM)] * len(blocks),
        out_shape=[jax.ShapeDtypeStruct(b.shape[1:], jnp.float32) for b in blocks],
        scratch_shapes=sums_scratch(blocks),
        compiler_params=pltpu.CompilerParams(
            collective_id=1, has_side_effects=True, vmem_limit_bytes=44 << 20
        ),
        name="scatter",
    )(*blocks)


def as_blocks(grad):
    return grad.astype(jnp.bfloat16).reshape(lax.axis_size("fsdp"), -1, grad.shape[1])


def sum_tp(part):
    part = part.astype(jnp.bfloat16)
    other = lax.ppermute(part, "tp", swapped)
    return part.astype(jnp.float32) + other.astype(jnp.float32)


def take_sequence(blocks):
    c = lax.axis_index("ctx")
    own = lax.dynamic_index_in_dim(blocks, c, 0, keepdims=False)
    give = lax.dynamic_index_in_dim(blocks, 1 - c, 0, keepdims=False)
    return jnp.concatenate([own, lax.ppermute(give, "ctx", swapped)], axis=0)


def give_back(own, came):
    c = lax.axis_index("ctx")
    return jnp.where(c == 0, jnp.stack([own, came]), jnp.stack([came, own]))


def dot(a, b, over):
    return lax.dot_general(a, b, (over, ((), ())), preferred_element_type=jnp.float32)


def turn(u):
    lane = lax.broadcasted_iota(jnp.int32, u.shape, 1)
    return jnp.where(lane % HD < HD // 2, -pltpu.roll(u, 96, 1), pltpu.roll(u, 32, 1))


def attend_kernel(*refs, tile):
    h_ref, w_ref, cos_ref, sin_ref = refs[:4]
    shards = refs[4:7]
    q_ref, k_ref, v_ref, o_ref, lse_ref = refs[7:12]
    wholes = refs[12:15]
    send, recv, local = refs[15:]
    copies = []
    for n in range(3):
        copies += gather_copies(shards[n], wholes[n], send.at[n], recv.at[n], local.at[n])

    @pl.when(pl.program_id(0) == 0)
    def _():
        greet(False)
        for copy in copies:
            copy.start()

    rows = h_ref.shape[0]
    raw = jnp.dot(h_ref[...], w_ref[...], preferred_element_type=jnp.float32)
    cosine, sine = cos_ref[...], sin_ref[...]
    q_raw, k_raw = raw[:, :128], raw[:, 128:256]
    q_ref[...] = (q_raw * cosine + turn(q_raw) * sine).astype(jnp.bfloat16)
    k_ref[...] = (k_raw * cosine + turn(k_raw) * sine).astype(jnp.bfloat16)
    v = raw[:, 256:]
    v_ref[...] = v.astype(jnp.bfloat16)
    v_turned = v.T.astype(jnp.bfloat16)
    k = k_ref[...]
    lane = lax.broadcasted_iota(jnp.int32, (tile, 128), 1)
    for start in range(0, rows, tile):
        at = slice(start, start + tile)
        q = q_ref[at, :] * jnp.bfloat16(HD ** (-0.5))
        outs = []
        for head in range(2):
            mine = (lane // HD) == head
            qm = jnp.where(mine, q, jnp.zeros_like(q))
            s = dot(k, qm, ((1,), (1,)))
            top = jnp.max(s, axis=0, keepdims=True)
            e = jnp.exp(s - top)
            total = jnp.sum(e, axis=0, keepdims=True)
            lse_ref[0, head : head + 1, at] = top + jnp.log(total)
            vh = v_turned[head * HD : (head + 1) * HD]
            outs.append(dot(vh, e.astype(jnp.bfloat16), ((1,), (0,))) / total)
        o_ref[at, :] = jnp.concatenate(outs, axis=0).T.astype(jnp.bfloat16)

    @pl.when(pl.program_id(0) == pl.num_programs(0) - 1)
    def _():
        for copy in copies:
            copy.wait()


def attend_back_kernel(*refs, tile):
    q_ref, k_ref, v_ref, o_ref, do_ref, lse_ref, cos_ref, sin_ref = refs[:8]
    out_ref = refs[11]
    dk_ref, dv_ref = refs[15:17]
    copies, groups, ctx_send, ctx_recv = sums_parts(refs[8:11], refs[12:15], refs[17:])

    @pl.when(pl.program_id(0) == 0)
    def _():
        greet(True)
        for copy in copies:
            copy.start()

    rows = q_ref.shape[0]
    k, v = k_ref[...], v_ref[...]
    k_turned = k.astype(jnp.float32).T.astype(jnp.bfloat16)
    lane = lax.broadcasted_iota(jnp.int32, (tile, 128), 1)
    dk_ref[...] = jnp.zeros_like(dk_ref)
    dv_ref[...] = jnp.zeros_like(dv_ref)
    for start in range(0, rows, tile):
        at = slice(start, start + tile)
        q = q_ref[at, :] * jnp.bfloat16(HD ** (-0.5))
        do = do_ref[at, :]
        prod = (do.astype(jnp.float32) * o_ref[at, :].astype(jnp.float32)).T
        outs = []
        for head in range(2):
            mine = (lane // HD) == head
            qm = jnp.where(mine, q, jnp.zeros_like(q))
            dm = jnp.where(mine, do, jnp.zeros_like(do))
            delta = jnp.sum(prod[head * HD : (head + 1) * HD], axis=0, keepdims=True)
            p = jnp.exp(dot(k, qm, ((1,), (1,))) - lse_ref[0, head : head + 1, at])
            ds = (p * (dot(v, dm, ((1,), (1,))) - delta)).astype(jnp.bfloat16)
            dv_ref[...] += dot(p.astype(jnp.bfloat16), dm, ((1,), (0,)))
            dk_ref[...] += dot(ds, qm, ((1,), (0,)))
            outs.append(dot(k_turned[head * HD : (head + 1) * HD], ds, ((1,), (0,))))
        dq = jnp.concatenate(outs, axis=0).T * (HD ** (-0.5))
        dq = dq * cos_ref[at, :] - turn(dq) * sin_ref[at, :]
        out_ref[at, :128] = dq.astype(jnp.bfloat16)
    dk = dk_ref[...]
    out_ref[:, 128:256] = (dk * cos_ref[...] - turn(dk) * sin_ref[...]).astype(jnp.bfloat16)
    out_ref[:, 256:] = dv_ref[...].astype(jnp.bfloat16)

    @pl.when(pl.program_id(0) == pl.num_programs(0) - 1)
    def _():
        for copy in copies:
            copy.wait()
        finish_sums(groups, ctx_send, ctx_recv)


def attend(h_one, w_pairs, cosine, sine, *shards):
    count = lax.axis_size("fsdp")
    anywhere = [pl.BlockSpec(memory_space=pl.ANY)] * len(shards)
    rows, model = h_one.shape
    pairs = w_pairs.shape[1] // 384
    width = pairs * 128
    column = pl.BlockSpec((rows, 128), lambda i: (0, i))
    table = pl.BlockSpec((rows, 128), lambda i: (0, 0))
    low = jax.ShapeDtypeStruct((rows, width), jnp.bfloat16)
    return pl.pallas_call(
        partial(attend_kernel, tile=min(512, rows)),
        grid=(pairs,),
        in_specs=[
            pl.BlockSpec((rows, model), lambda i: (0, 0)),
            pl.BlockSpec((model, 384), lambda i: (0, i)),
            table,
            table,
        ]
        + anywhere,
        out_specs=[column] * 4 + [pl.BlockSpec((1, 2, rows), lambda i: (i, 0, 0))] + anywhere,
        out_shape=[low] * 4
        + [jax.ShapeDtypeStruct((pairs, 2, rows), jnp.float32)]
        + [jax.ShapeDtypeStruct((count,) + s.shape, s.dtype) for s in shards],
        scratch_shapes=semaphores(len(shards), count),
        compiler_params=pltpu.CompilerParams(
            collective_id=2, has_side_effects=True, vmem_limit_bytes=44 << 20
        ),
        cost_estimate=pl.CostEstimate(
            flops=16 * 10**9, bytes_accessed=10**7, transcendentals=pairs * 2 * rows * rows
        ),
        name="attend",
    )(h_one, w_pairs, cosine, sine, *shards)


def attend_back(q, k, v, o, do, lse, cosine, sine, *blocks):
    rows, width = q.shape
    pairs = width // 128
    column = pl.BlockSpec((rows, 128), lambda i: (0, i))
    table = pl.BlockSpec((rows, 128), lambda i: (0, 0))
    return pl.pallas_call(
        partial(attend_back_kernel, tile=min(512, rows)),
        grid=(pairs,),
        in_specs=[column] * 5
        + [pl.BlockSpec((1, 2, rows), lambda i: (i, 0, 0)), table, table]
        + [pl.BlockSpec(memory_space=pl.ANY)] * len(blocks),
        out_specs=[pl.BlockSpec((rows, 384), lambda i: (0, i))]
        + [pl.BlockSpec(b.shape[1:], lambda i: (0, 0)) for b in blocks],
        out_shape=[jax.ShapeDtypeStruct((rows, 3 * width), jnp.bfloat16)]
        + [jax.ShapeDtypeStruct(b.shape[1:], jnp.float32) for b in blocks],
        scratch_shapes=[pltpu.VMEM((rows, 128), jnp.float32)] * 2 + sums_scratch(blocks),
        compiler_params=pltpu.CompilerParams(
            collective_id=3, has_side_effects=True, vmem_limit_bytes=48 << 20
        ),
        cost_estimate=pl.CostEstimate(
            flops=30 * 10**9, bytes_accessed=10**7, transcendentals=pairs * 2 * rows * rows
        ),
        name="attend_back",
    )(q, k, v, o, do, lse, cosine, sine, *blocks)


def rope_tables(rows):
    angle = np.arange(2 * rows, dtype=np.float32)[:, None] * (
        np.float32(1.0)
        / np.float32(rope_base) ** (np.arange(0, HD, 2, dtype=np.float32) / np.float32(HD))
    )[None, :].astype(np.float32)
    tables = []
    for values in (np.cos(angle), np.sin(angle)):
        whole = jnp.asarray(np.tile(values.astype(np.float32), (1, 4)))
        flipped = jnp.concatenate([whole[rows:], whole[:rows]], axis=0)
        tables.append(jnp.where(lax.axis_index("ctx") == 0, whole, flipped))
    return tables


def on_device(
    tokens, gain_attn, w_query, w_key, w_value, w_out, gain_ffn, w_gate, w_up, w_down, cotangent
):
    slots, rows, model = tokens.shape
    part = w_query.shape[0]
    width = w_query.shape[1]
    pairs = width // 128
    units = w_gate.shape[1]
    packed = jnp.stack(
        [w.reshape(part, pairs, 128) for w in (w_query, w_key, w_value)], axis=2
    ).reshape(part, 3 * width)
    gains = jnp.pad(
        jnp.stack([gain_attn, gain_ffn]).astype(jnp.float32), ((0, 6), (0, 128 - part))
    )
    x = take_sequence(tokens).astype(jnp.float32)
    qkv_w, gains = gather(packed, gains)
    qkv_w = qkv_w.reshape(model, -1)
    gain_one, gain_two = gains[:, 0, :part].reshape(-1), gains[:, 1, :part].reshape(-1)
    cotangent, _ = lax.optimization_barrier((cotangent, qkv_w))
    grad_low = take_sequence(cotangent)
    grad_y = grad_low.astype(jnp.float32)
    cosine, sine = rope_tables(rows)

    normed_one, rstd_one = layer_norm(x)
    h_one = (normed_one * gain_one).astype(jnp.bfloat16)
    shards = (w_out.T, jnp.concatenate([w_gate, w_up], axis=1), w_down.T)
    q, k, v, attended, lse, *rest = attend(h_one, qkv_w, cosine, sine, *shards)
    out_w, ffn_w, down_w = (w.reshape(model, -1) for w in rest)
    x_two = x + sum_tp(dot(attended, out_w, ((1,), (1,))))
    normed_two, rstd_two = layer_norm(x_two)
    h_two = (normed_two * gain_two).astype(jnp.bfloat16)
    both = matmul(h_two, ffn_w)
    gate, up_part = both[:, :units], both[:, units:]
    activated, gelu_back = jax.vjp(partial(jax.nn.gelu, approximate=False), gate)
    hidden = (activated * up_part).astype(jnp.bfloat16)
    output = (x_two + sum_tp(dot(hidden, down_w, ((1,), (1,))))).astype(jnp.bfloat16)
    output = give_back(output[:rows], lax.ppermute(output[rows:], "ctx", swapped))

    grad_hidden = matmul(grad_low, down_w)
    grad_both = jnp.concatenate(
        [
            gelu_back(grad_hidden * up_part)[0].astype(jnp.bfloat16),
            (grad_hidden * activated).astype(jnp.bfloat16),
        ],
        axis=1,
    )
    grad_h_two = sum_tp(dot(grad_both, ffn_w, ((1,), (1,))))
    ffn_blocks = as_blocks(dot(h_two, grad_both, ((0,), (0,))))
    down_blocks = as_blocks(dot(grad_low, hidden, ((0,), (0,))))
    grad_gain_ffn = jnp.sum(grad_h_two * normed_two, axis=0)
    grad_x_two = grad_y + norm_back(grad_h_two * gain_two, normed_two, rstd_two)
    branch_low = grad_x_two.astype(jnp.bfloat16)
    out_blocks = as_blocks(dot(branch_low, attended, ((0,), (0,))))
    grad_att = matmul(branch_low, out_w).astype(jnp.bfloat16)
    grad_qkv, own_ffn, own_down, own_out = attend_back(
        q, k, v, attended, grad_att, lse, cosine, sine, ffn_blocks, down_blocks, out_blocks
    )
    grad_h_one = sum_tp(dot(grad_qkv, qkv_w, ((1,), (1,))))
    qkv_blocks = as_blocks(dot(h_one, grad_qkv, ((0,), (0,))))
    grad_gain_attn = jnp.sum(grad_h_one * normed_one, axis=0)
    grad_x = grad_x_two + norm_back(grad_h_one * gain_one, normed_one, rstd_one)
    came = lax.ppermute(grad_x[rows:].astype(jnp.bfloat16), "ctx", swapped).astype(jnp.float32)
    grad_tokens = give_back(grad_x[:rows], came)
    gain_blocks = jnp.pad(
        jnp.stack([grad_gain_attn, grad_gain_ffn]).reshape(2, -1, part).transpose(1, 0, 2),
        ((0, 0), (0, 6), (0, 128 - part)),
    )
    own_qkv, own_gains = scatter(qkv_blocks, gain_blocks)
    own_gains = own_gains[:, :part]
    own_qkv = own_qkv.reshape(part, pairs, 3, 128)
    return (
        output,
        grad_tokens,
        own_gains[0],
        own_qkv[:, :, 0].reshape(part, width),
        own_qkv[:, :, 1].reshape(part, width),
        own_qkv[:, :, 2].reshape(part, width),
        own_out.T,
        own_gains[1],
        own_ffn[:, :units],
        own_ffn[:, units:],
        own_down.T,
    )


def solution(mesh):
    whole = mesh.shape["ctx"] == 2 and mesh.shape["tp"] == 2
    step = on_device if whole and mesh.shape["fsdp"] == 8 else on_device_blocks
    placed = (
        P(None, ("fsdp", "ctx"), None),
        P("fsdp"),
        P("fsdp", "tp"),
        P("fsdp", "tp"),
        P("fsdp", "tp"),
        P("tp", "fsdp"),
        P("fsdp"),
        P("fsdp", "tp"),
        P("fsdp", "tp"),
        P("tp", "fsdp"),
        P(None, ("fsdp", "ctx"), None),
    )
    return jax.shard_map(
        step,
        mesh=mesh,
        in_specs=placed,
        out_specs=(
            P(None, ("fsdp", "ctx"), None),
            P(None, ("fsdp", "ctx"), None),
            P("fsdp"),
            P("fsdp", "tp"),
            P("fsdp", "tp"),
            P("fsdp", "tp"),
            P("tp", "fsdp"),
            P("fsdp"),
            P("fsdp", "tp"),
            P("fsdp", "tp"),
            P("tp", "fsdp"),
        ),
        check_vma=False,
    )
```
